128 devices in a mesh: group: 16 (over x, z), tensor: 8 (over y, core).
Axes of the slice: x: 4, y: 4, z: 4, core: 2. Of those that a mesh axis runs over, the one named last changes fastest.
Arguments:
- queries: bfloat16 [16384, 4096], P(('group', 'tensor')), may hold values from -6 to 6
- rotated_key_rows: bfloat16 [16384, 256], P(('group', 'tensor')), may hold values from -6 to 6
- value_row_matrix: bfloat16 [16384, 256], P(('group', 'tensor')), may hold values from -12 to 12
- out_weight: bfloat16 [4096, 4096], P('tensor'), may hold values from -0.09375 to 0.09375
- residual: bfloat16 [16384, 4096], P(('group', 'tensor')), may hold values from -3 to 3
- norm_gain: float32 [4096], replicated, may hold values from 0.25 to 1.75
- expert_ids: int32 [16384, 3], P(('group', 'tensor')), may hold values from 0 to 63, all different within a row; in each aligned block of 128 rows (0 to 127, 128 to 255, ...) at most 8 rows name the same one
- gate_weights: float32 [16384, 3], P(('group', 'tensor')), may hold values from 0.05 to 0.6
- w_gate: bfloat16 [128, 4096, 768], P(('group', 'tensor')), may hold values from -0.09375 to 0.09375
- w_up: bfloat16 [128, 4096, 768], P(('group', 'tensor')), may hold values from -0.09375 to 0.09375
- w_down: bfloat16 [128, 768, 4096], P(('group', 'tensor')), may hold values from -0.15625 to 0.15625
Outputs:
- mixed: bfloat16 [16384, 4096], P(('group', 'tensor'))
The draws below stay inside these ranges and needn't reach their ends.
Inputs may be any that keep to these rules, and one draw needn't show every extreme that they name: `expert_ids`: the 3 experts of a row differ. Among the 128 rows of one device (aligned blocks), at most 8 name one expert, and in every draw some expert is named by exactly 8 of them.
All inputs are finite; a program needn't handle non-finite values.
Results may differ from the reference program's by a relative error of at most 0.0065.
Values may be sent and summed in bfloat16 or wider, within the bound.
No kernel may reach another device: no remote copies, remote signals or barrier semaphores. Data moves between devices by JAX's collectives and lax.ppermute only.
A program may use at most 128 MiB of HBM per device.

```python
import math
import jax
import jax.numpy as jnp
import numpy as np
from jax import lax

D = 4096
FF = 1536
QUERY_HEADS = 32
KEY_VALUE_HEADS = 2
HEAD_SIZE = 128
TOP = 3
TOK_DEV = 128
PREFILL_SPAN = 1024
TOKEN_TOTAL = 16384
EXPERTS = 64
CAP = 8
N_GROUP = 16
N_TENSOR = 8


def draw_queries(key, part):
    key = jax.random.fold_in(key, 11)
    return jnp.clip(jax.random.normal(jax.random.fold_in(key, 1), (TOKEN_TOTAL, QUERY_HEADS * HEAD_SIZE), jnp.float32), -6.0, 6.0).astype(jnp.bfloat16)


def draw_rotated_key_rows(key, part):
    key = jax.random.fold_in(key, 13)
    return jnp.clip(jax.random.normal(jax.random.fold_in(key, 1), (TOKEN_TOTAL, KEY_VALUE_HEADS * HEAD_SIZE), jnp.float32), -6.0, 6.0).astype(jnp.bfloat16)


def level_of(key, extent, cuts, low, high):
    loudness = 1.0
    for position, parts in cuts:
        heights = jax.random.uniform(jax.random.fold_in(jax.random.fold_in(key, 6), position), (parts,), jnp.float32, low / len(cuts), high / len(cuts))
        loudness = loudness * jnp.repeat(jnp.exp(heights), extent[position] // parts).reshape((-1,) + (1,) * (len(extent) - 1 - position))
    return loudness


def assign_block(stream_key, own, number, rows, number_of, top, bound, skew):
    ranking = jax.random.permutation(stream_key, number_of)
    packed, common = shares(number_of, rows * top, bound, skew, True), shares(number_of, rows * top, bound, skew, False)
    places = jnp.arange(number_of)

    def named(sizes, turn):
        used = int((sizes > 0).sum())
        fixed = max(1, used // 4)
        passed = fixed + (places - fixed + turn * (used - fixed)) % max(1, number_of - fixed)
        return jnp.zeros((number_of,), jnp.int32).at[ranking[jnp.where(places < fixed, places, passed)]].set(jnp.asarray(sizes, jnp.int32))

    sizes = jnp.where(number % 4 == 0, named(packed, number // 4), named(common, number - number // 4 - 1))
    mixed = jax.random.permutation(jax.random.fold_in(own, 3), number_of)
    giver, receiver = mixed[0:number_of // 2 * 2:2], mixed[1:number_of // 2 * 2:2]
    room = jnp.minimum(sizes[giver] - 1, bound - sizes[receiver]) // 2
    room = jnp.where((giver == ranking[0]) | (receiver == ranking[0]) | (sizes[receiver] == 0), 0, jnp.maximum(room, 0))
    passed = jax.random.randint(jax.random.fold_in(own, 4), (number_of // 2,), 0, 1 << 20) % (room + 1)
    sizes = sizes.at[giver].add(-passed).at[receiver].add(passed)
    items = jnp.searchsorted(jnp.cumsum(sizes), jnp.arange(rows * top), side="right").astype(jnp.int32)
    grid = items.reshape(top, rows).T
    grid = grid[jax.random.permutation(jax.random.fold_in(own, 1), rows)]
    turn = jax.random.randint(jax.random.fold_in(own, 2), (rows, 1), 0, top)
    return jnp.take_along_axis(grid, (jnp.arange(top)[None, :] + turn) % top, axis=1)


def shares(count, total, reach, skew, full):
    weights = [(1 << 20) // math.isqrt(rank ** skew) + 1 for rank in range(1, count + 1)]
    largest = reach if full else min(reach, max(-(-total // count), total * weights[0] // sum(weights)))
    least = 1 if total - largest >= count - 1 else 0
    holding, surplus = [largest] + [least] * (count - 1), total - largest - least * (count - 1)
    while surplus > 0:
        candidates = [i for i in range(1, count) if holding[i] < largest] or [i for i in range(1, count) if holding[i] < reach]
        pool, left = sum([weights[i] for i in candidates]), surplus
        for i in candidates:
            extra = min(reach - holding[i], max(1, left * weights[i] // pool), surplus)
            holding[i] = holding[i] + extra
            surplus = surplus - extra
    return np.array(holding)


def normal_values(own_key, extent, scale, reach, shards=(), kind=jnp.bfloat16):
    values = jax.random.normal(own_key, extent, jnp.float32) * scale
    if len(shards) > 0:
        values = level_of(own_key, extent, shards, -0.22, 0.18) * values
    return jnp.clip(values, min=-reach, max=reach).astype(kind)


def setup_inputs(seed: int = 0) -> dict:
    key_of = jax.random.split(jax.random.key(seed), 12)
    queries = draw_queries(jax.random.fold_in(key_of[11], 71), 0)
    rotated_key_rows = draw_rotated_key_rows(jax.random.fold_in(key_of[11], 71), 0)
    value_row_matrix = normal_values(key_of[2], (TOKEN_TOTAL, KEY_VALUE_HEADS * HEAD_SIZE), 2.0, 12.0, ((0, 128),))
    out_weight = normal_values(key_of[3], (QUERY_HEADS * HEAD_SIZE, D), (QUERY_HEADS * HEAD_SIZE) ** -0.5, 0.09375, ((0, 8),))
    residual = normal_values(key_of[4], (TOKEN_TOTAL, D), 0.5, 3.0, ((0, 128),))
    norm_gain = jnp.clip(1.0 + 0.15 * jax.random.normal(key_of[5], (D,), jnp.float32), 0.25, 1.75)
    expert_ids_keys = jax.random.split(jax.random.fold_in(key_of[6], 1), TOKEN_TOTAL // TOK_DEV)
    expert_ids_turns = jax.random.permutation(jax.random.fold_in(key_of[6], 3), TOKEN_TOTAL // TOK_DEV)
    expert_ids = jax.vmap(lambda own, number: assign_block(jax.random.fold_in(key_of[6], 2), own, number, TOK_DEV, EXPERTS, TOP, CAP, 2))(expert_ids_keys, expert_ids_turns).reshape((TOKEN_TOTAL, TOP))
    gate_weights = jnp.clip(jnp.exp(math.log(0.6) - 2.4849067 * jax.random.uniform(key_of[7], (TOKEN_TOTAL, TOP), jnp.float32) ** level_of(key_of[7], (TOKEN_TOTAL, TOP), ((0, 128),), -0.2, 0.2)), 0.05, 0.6)
    w_gate = normal_values(key_of[8], (2 * EXPERTS, D, FF // 2), D ** -0.5, 0.09375, ((0, 128),))
    w_up = normal_values(key_of[9], (2 * EXPERTS, D, FF // 2), D ** -0.5, 0.09375, ((0, 128),))
    w_down = normal_values(key_of[10], (2 * EXPERTS, FF // 2, D), FF ** -0.5, 0.15625, ((0, 128),))
    return {"queries": queries, "rotated_key_rows": rotated_key_rows, "value_row_matrix": value_row_matrix, "out_weight": out_weight, "residual": residual, "norm_gain": norm_gain, "expert_ids": expert_ids, "gate_weights": gate_weights, "w_gate": w_gate, "w_up": w_up, "w_down": w_down}


def attend_block(query_tile, key_tile, value_tile):
    row_total = query_tile.shape[0]
    grouped_queries = query_tile.reshape(row_total, KEY_VALUE_HEADS, QUERY_HEADS // KEY_VALUE_HEADS, HEAD_SIZE).astype(jnp.float32)
    key_broadcast = key_tile.reshape(row_total, KEY_VALUE_HEADS, HEAD_SIZE).astype(jnp.float32)
    value_broadcast = value_tile.reshape(row_total, KEY_VALUE_HEADS, HEAD_SIZE).astype(jnp.float32)
    scores = jnp.einsum('rkgd,ckd->kgrc', grouped_queries, key_broadcast) * HEAD_SIZE ** (-0.5)
    positions = jnp.arange(row_total, dtype=jnp.int32)
    allowed = positions[None, :] <= positions[:, None]
    scores = jnp.where(allowed, scores, -1e+30)
    largest = lax.optimization_barrier(jnp.max(scores, axis=-1, keepdims=True))
    weights = jnp.exp(scores - largest)
    probs = (weights / lax.optimization_barrier(jnp.sum(weights, axis=-1, keepdims=True))).astype(jnp.bfloat16)
    probs = lax.optimization_barrier(probs)
    context = jnp.einsum('kgrc,ckd->rkgd', probs.astype(jnp.float32), value_broadcast)
    return context.astype(jnp.bfloat16).reshape(row_total, QUERY_HEADS * HEAD_SIZE)

def reference(queries, rotated_key_rows, value_row_matrix, out_weight, residual, norm_gain, expert_ids, gate_weights, w_gate, w_up, w_down):
    block_count = TOKEN_TOTAL // PREFILL_SPAN
    block_list = (queries.reshape(block_count, PREFILL_SPAN, QUERY_HEADS * HEAD_SIZE), rotated_key_rows.reshape(block_count, PREFILL_SPAN, KEY_VALUE_HEADS * HEAD_SIZE), value_row_matrix.reshape(block_count, PREFILL_SPAN, KEY_VALUE_HEADS * HEAD_SIZE))
    context = lax.map(lambda items: attend_block(items[0], items[1], items[2]), block_list).reshape(TOKEN_TOTAL, QUERY_HEADS * HEAD_SIZE)
    projected = jnp.dot(context, out_weight, preferred_element_type=jnp.float32)
    hidden_state = residual.astype(jnp.float32) + projected
    mean_square = lax.optimization_barrier(jnp.mean(hidden_state * hidden_state, axis=-1, keepdims=True))
    moe_input = (hidden_state * lax.rsqrt(mean_square + 1e-06) * norm_gain).astype(jnp.bfloat16)
    most = N_GROUP * N_TENSOR * CAP

    def one_expert(total, expert):
        chosen = expert_ids == expert
        weight = lax.optimization_barrier(jnp.sum(jnp.where(chosen, gate_weights, 0.0), axis=1))
        member = jnp.any(chosen, axis=1)
        picked = jnp.nonzero(member, size=most, fill_value=0)[0].astype(jnp.int32)
        valid = jnp.arange(most, dtype=jnp.int32) < jnp.sum(member.astype(jnp.int32))
        rows_in = moe_input[picked]
        pieces = []
        for half in range(2):
            index = 2 * expert + half
            gate = jnp.dot(rows_in, w_gate[index], preferred_element_type=jnp.float32)
            upward = jnp.dot(rows_in, w_up[index], preferred_element_type=jnp.float32)
            activation = (jax.nn.silu(gate) * upward).astype(jnp.bfloat16)
            piece = jnp.dot(activation, w_down[index], preferred_element_type=jnp.float32).astype(jnp.bfloat16)
            pieces.append(lax.optimization_barrier(piece))
        merged = (pieces[0].astype(jnp.float32) + pieces[1].astype(jnp.float32)).astype(jnp.bfloat16)
        merged = lax.optimization_barrier(merged)
        factor = jnp.where(valid, weight[picked], 0.0)
        return (total.at[picked].add(merged.astype(jnp.float32) * factor[:, None]), None)
    start = jnp.zeros((TOKEN_TOTAL, D), jnp.float32)
    routed, _ = lax.scan(one_expert, start, jnp.arange(EXPERTS, dtype=jnp.int32))
    return (hidden_state + routed).astype(jnp.bfloat16)
```

```python
import jax
import jax.numpy as jnp
from jax import lax
from jax.experimental import pallas as pl
from jax.experimental.pallas import tpu as pltpu
from jax.sharding import PartitionSpec as P

HEAD = 128
TOP = 3
CAP = 8
AXES = ("group", "tensor")
LOG2E = 1.4426950408889634
ORDER = (2, 1, 3, 0)


def attention_kernel(where_ref, q_ref, k_ref, v_ref, o_ref):
    rows = q_ref.shape[1]
    heads = q_ref.shape[2] // HEAD
    place = where_ref[pl.program_id(0)]
    core = where_ref[4]
    scale = HEAD ** (-0.5) * LOG2E
    for block in range(4):

        @pl.when(place == block)
        def _():
            columns = 256 * (block + 1)
            keys = k_ref[0:columns, :]
            values = v_ref[0:columns, :]
            row = lax.broadcasted_iota(jnp.int32, (2 * rows, 256), 0) % rows
            column = lax.broadcasted_iota(jnp.int32, (2 * rows, 256), 1)
            allowed = column <= row + core * rows

            def pair(index, carry):
                start = pl.multiple_of(index * 2 * HEAD, 2 * HEAD)
                both = q_ref[0, :, pl.ds(start, 2 * HEAD)]
                q = jnp.concatenate([both[:, :HEAD], both[:, HEAD:]], axis=0)
                scores = lax.dot_general(
                    q, keys, (((1,), (1,)), ((), ())), preferred_element_type=jnp.float32
                )
                last = jnp.where(allowed, scores[:, columns - 256 :], -1e30)
                if block:
                    scores = jnp.concatenate([scores[:, : columns - 256], last], axis=1)
                else:
                    scores = last
                largest = jnp.max(scores, axis=1, keepdims=True)
                weights = jnp.exp2((scores - largest) * scale)
                total = jnp.sum(weights, axis=1, keepdims=True)
                context = jnp.dot(
                    weights.astype(jnp.bfloat16), values, preferred_element_type=jnp.float32
                )
                context = (context / total).astype(jnp.bfloat16)
                o_ref[0, :, pl.ds(start, 2 * HEAD)] = jnp.concatenate(
                    [context[:rows], context[rows:]], axis=1
                )
                return carry

            lax.fori_loop(0, heads // 2, pair, 0)


def attention(where, queries, keys, values):
    ring, rows, width = queries.shape
    return pl.pallas_call(
        attention_kernel,
        out_shape=jax.ShapeDtypeStruct((ring, rows, width), jnp.bfloat16),
        grid_spec=pltpu.PrefetchScalarGridSpec(
            num_scalar_prefetch=1,
            grid=(ring,),
            in_specs=[
                pl.BlockSpec((1, rows, width), lambda i, w: (i, 0, 0)),
                pl.BlockSpec(keys.shape, lambda i, w: (0, 0)),
                pl.BlockSpec(values.shape, lambda i, w: (0, 0)),
            ],
            out_specs=pl.BlockSpec((1, rows, width), lambda i, w: (i, 0, 0)),
        ),
        compiler_params=pltpu.CompilerParams(vmem_limit_bytes=32 * 1024 * 1024),
        cost_estimate=pl.CostEstimate(
            flops=2 * 2 * 8 * rows * 2560 * HEAD, bytes_accessed=3 << 20, transcendentals=8 * rows * 2560
        ),
    )(where, queries, keys, values)


def fdot(a, b):
    return jnp.dot(a, b, preferred_element_type=jnp.float32)


def local(
    queries,
    rotated_key_rows,
    value_row_matrix,
    out_weight,
    residual,
    norm_gain,
    expert_ids,
    gate_weights,
    w_gate,
    w_up,
    w_down,
):
    bf16, f32 = jnp.bfloat16, jnp.float32
    rows = queries.shape[0]
    width = residual.shape[1]
    tensor = lax.axis_size("tensor")
    devices = lax.axis_size("group") * tensor
    experts = devices // 2
    place = lax.axis_index("tensor")
    y, core = place // 2, place % 2
    other = 1 - core
    ring = tensor // 2
    chip_width = queries.shape[1] // ring
    half_width = chip_width // 2
    half = width // 2

    def along(value, step):
        return lax.ppermute(value, "tensor", [(i, (i + 2 * step) % tensor) for i in range(tensor)])

    def swap(value):
        return lax.ppermute(value, "tensor", [(i, i ^ 1) for i in range(tensor)])

    def columns(value, start, size):
        return lax.dynamic_slice_in_dim(value, start, size, axis=1)

    weight_other = swap(out_weight)

    def outgoing(step):
        to = (y + step) % ring
        key_head = to * rotated_key_rows.shape[1] // HEAD // ring * HEAD
        return jnp.concatenate(
            [
                columns(queries, to * chip_width + core * half_width, half_width),
                columns(queries, to * chip_width + other * half_width, half_width),
                columns(rotated_key_rows, key_head, HEAD),
                columns(value_row_matrix, key_head, HEAD),
            ],
            axis=1,
        )

    arrived = [outgoing(0)] + [along(outgoing(step), step) for step in (1, 2, 3)]
    stacked = jnp.stack([arrived[(-s) % ring] for s in ORDER])
    key_values = stacked[:, :, chip_width:]
    key_values_other = swap(key_values)
    places = (y + jnp.array(ORDER, jnp.int32)) % ring
    gathered = jnp.where(
        core == 0,
        jnp.stack([key_values, key_values_other], axis=1),
        jnp.stack([key_values_other, key_values], axis=1),
    )
    slot_of = jnp.array([ORDER.index(s) for s in range(ring)], jnp.int32)
    gathered = jnp.take(gathered, jnp.take(slot_of, (jnp.arange(ring) - y) % ring), axis=0)
    gathered = gathered.reshape(ring * 2 * rows, 2 * HEAD)
    where = jnp.concatenate([places, core[None]]).astype(jnp.int32)
    context = attention(where, stacked[:, :, :chip_width], gathered[:, :HEAD], gathered[:, HEAD:])

    def project(block):
        return fdot(block[:, :half_width], out_weight) + fdot(block[:, half_width:], weight_other)

    opposite = project(context[0]).astype(bf16)
    from_left = along(opposite[:, :half], 1)
    from_right = along(opposite[:, half:], -1)
    right = project(context[1])
    left = project(context[2])
    right_plain = along(right[:, half:].astype(bf16), 1)
    left_plain = along(left[:, :half].astype(bf16), -1)
    right_sum = along((right[:, :half] + from_left.astype(f32)).astype(bf16), 1)
    left_sum = along((left[:, half:] + from_right.astype(f32)).astype(bf16), -1)
    own = project(context[3])
    hidden = residual.astype(f32) + own
    hidden = hidden + jnp.concatenate(
        [
            right_sum.astype(f32) + left_plain.astype(f32),
            right_plain.astype(f32) + left_sum.astype(f32),
        ],
        axis=1,
    )

    mean_square = jnp.mean(hidden * hidden, axis=-1, keepdims=True)
    moe_input = (hidden * lax.rsqrt(mean_square + 1e-06) * norm_gain).astype(bf16)

    flat_ids = expert_ids.reshape(-1)
    one_hot = (flat_ids[:, None] == jnp.arange(experts, dtype=jnp.int32)[None, :]).astype(jnp.int32)
    earlier = jnp.cumsum(one_hot, axis=0) - one_hot
    rank_within = jnp.sum(earlier * one_hot, axis=1)
    slot_index = (flat_ids * (2 * CAP) + rank_within).reshape(rows, TOP)
    slot_rows = jnp.arange(2 * experts * CAP, dtype=jnp.int32)[:, None]
    hit = [
        [slot_rows == slot_index[:, k][None, :] + side * CAP for k in range(TOP)] for side in (0, 1)
    ]
    selector = jnp.concatenate([h[0] | h[1] | h[2] for h in hit], axis=1).astype(bf16)
    spread = jnp.concatenate(
        [
            sum(jnp.where(h[k], gate_weights[:, k][None, :], 0.0) for k in range(TOP))
            for h in hit
        ],
        axis=1,
    )
    spread_high = spread.astype(bf16)
    spread_low = (spread - spread_high.astype(f32)).astype(bf16)

    halves = jnp.concatenate([moe_input[:, :half], moe_input[:, half:]], axis=0)
    slots = fdot(selector, halves).astype(bf16).reshape(devices, CAP, half)
    mine = lax.all_to_all(slots, AXES, split_axis=0, concat_axis=0, tiled=True)
    mine = mine.reshape(devices * CAP, half)
    theirs = swap(mine)

    def rows_of(weight, side):
        return lax.dynamic_slice_in_dim(weight[0], side * half, half, axis=0)

    gate = fdot(mine, rows_of(w_gate, core))
    upward = fdot(mine, rows_of(w_up, core))
    gate = gate + fdot(theirs, rows_of(w_gate, other))
    upward = upward + fdot(theirs, rows_of(w_up, other))
    activation = (jax.nn.silu(gate) * upward).astype(bf16)
    to_other = fdot(activation, columns(w_down[0], other * half, half)).astype(bf16)
    part_other = swap(to_other)
    part_own = fdot(activation, columns(w_down[0], core * half, half)).astype(bf16)
    expert_out = (part_own.astype(f32) + part_other.astype(f32)).astype(bf16)
    returned = lax.all_to_all(
        expert_out.reshape(devices, CAP, half), AXES, split_axis=0, concat_axis=0, tiled=True
    ).reshape(devices * CAP, half)

    def gather_back(weights):
        return lax.dot_general(
            weights, returned, (((0,), (0,)), ((), ())), preferred_element_type=f32
        )

    routed = gather_back(spread_high) + gather_back(spread_low)
    routed = jnp.concatenate([routed[:rows], routed[rows:]], axis=1)
    return (hidden + routed).astype(bf16)


def solution(mesh):
    wide = P(AXES, None)
    return jax.shard_map(
        local,
        mesh=mesh,
        in_specs=(
            wide,
            wide,
            wide,
            P("tensor", None),
            wide,
            P(),
            wide,
            wide,
            P(AXES, None, None),
            P(AXES, None, None),
            P(AXES, None, None),
        ),
        out_specs=wide,
        check_vma=False,
    )
```

```python
import jax
import jax.numpy as jnp
from jax import lax
from jax.experimental import pallas as pl
from jax.experimental.pallas import tpu as pltpu
from jax.sharding import Mesh
from jax.sharding import PartitionSpec as P

HEAD = 128
TOP = 3
CAP = 8
AXES = ("group", "y", "core")
LOG2E = 1.4426950408889634
ORDER = (2, 1, 3, 0)


def attention_kernel(where_ref, q_ref, k_ref, v_ref, o_ref):
    rows = q_ref.shape[1]
    heads = q_ref.shape[2] // HEAD
    place = where_ref[pl.program_id(0)]
    core = where_ref[4]
    scale = HEAD ** (-0.5) * LOG2E
    for block in range(4):

        @pl.when(place == block)
        def _():
            columns = 256 * (block + 1)
            keys = k_ref[0:columns, :]
            values = v_ref[0:columns, :]
            row = lax.broadcasted_iota(jnp.int32, (2 * rows, 256), 0) % rows
            column = lax.broadcasted_iota(jnp.int32, (2 * rows, 256), 1)
            allowed = column <= row + core * rows

            for index in range(heads // 2):
                start = index * 2 * HEAD
                both = q_ref[0, :, start : start + 2 * HEAD]
                q = jnp.concatenate([both[:, :HEAD], both[:, HEAD:]], axis=0)
                scores = lax.dot_general(
                    q, keys, (((1,), (1,)), ((), ())), preferred_element_type=jnp.float32
                )
                last = jnp.where(allowed, scores[:, columns - 256 :], -1e30)
                if block:
                    scores = jnp.concatenate([scores[:, : columns - 256], last], axis=1)
                else:
                    scores = last
                largest = jnp.max(scores, axis=1, keepdims=True)
                weights = jnp.exp2((scores - largest) * scale).astype(jnp.bfloat16)
                context = jnp.dot(weights, values, preferred_element_type=jnp.float32)
                context = (context[:, :HEAD] / context[:, HEAD:]).astype(jnp.bfloat16)
                o_ref[0, :, start : start + 2 * HEAD] = jnp.concatenate(
                    [context[:rows], context[rows:]], axis=1
                )


def attention(where, queries, keys, values):
    ring, rows, width = queries.shape
    return pl.pallas_call(
        attention_kernel,
        out_shape=jax.ShapeDtypeStruct((ring, rows, width), jnp.bfloat16),
        grid_spec=pltpu.PrefetchScalarGridSpec(
            num_scalar_prefetch=1,
            grid=(ring,),
            in_specs=[
                pl.BlockSpec((1, rows, width), lambda i, w: (i, 0, 0)),
                pl.BlockSpec(keys.shape, lambda i, w: (0, 0)),
                pl.BlockSpec(values.shape, lambda i, w: (0, 0)),
            ],
            out_specs=pl.BlockSpec((1, rows, width), lambda i, w: (i, 0, 0)),
        ),
        compiler_params=pltpu.CompilerParams(vmem_limit_bytes=20 * 1024 * 1024),
        cost_estimate=pl.CostEstimate(
            flops=ring * 8 * rows * 2560 * HEAD, bytes_accessed=ring << 20, transcendentals=ring * 2 * rows * 2560
        ),
    )(where, queries, keys, values)


def fdot(a, b):
    return jnp.dot(a, b, preferred_element_type=jnp.float32)


def project_kernel(context_ref, own_ref, other_ref, o_ref):
    half = own_ref.shape[0]
    result = jnp.dot(
        context_ref[:, :half], own_ref[...], preferred_element_type=jnp.float32
    ) + jnp.dot(context_ref[:, half:], other_ref[...], preferred_element_type=jnp.float32)
    o_ref[...] = result.astype(o_ref.dtype)


def project(context, weight_own, weight_other, dtype, tile=1024):
    ring, rows, depth = context.shape
    context = context.reshape(ring * rows, depth)
    half, width = weight_own.shape
    return pl.pallas_call(
        project_kernel,
        out_shape=jax.ShapeDtypeStruct((ring * rows, width), dtype),
        grid=(width // tile,),
        in_specs=[
            pl.BlockSpec((ring * rows, depth), lambda j: (0, 0)),
            pl.BlockSpec((half, tile), lambda j: (0, j)),
            pl.BlockSpec((half, tile), lambda j: (0, j)),
        ],
        out_specs=pl.BlockSpec((ring * rows, tile), lambda j: (0, j)),
        compiler_params=pltpu.CompilerParams(vmem_limit_bytes=16 * 1024 * 1024),
        cost_estimate=pl.CostEstimate(
            flops=2 * ring * rows * depth * width, bytes_accessed=2 * depth * width, transcendentals=0
        ),
    )(context, weight_own, weight_other)


def gated_kernel(x_ref, gate_ref, up_ref, o_ref):
    x = x_ref[...]
    gate = jnp.dot(x, gate_ref[0], preferred_element_type=jnp.float32)
    upward = jnp.dot(x, up_ref[0], preferred_element_type=jnp.float32)
    o_ref[...] = (gate / (1.0 + jnp.exp(-gate)) * upward).astype(jnp.bfloat16)


def gated(x, w_gate, w_up, tile=256):
    rows, depth = x.shape
    hidden = w_gate.shape[2]
    return pl.pallas_call(
        gated_kernel,
        out_shape=jax.ShapeDtypeStruct((rows, hidden), jnp.bfloat16),
        grid=(hidden // tile,),
        in_specs=[
            pl.BlockSpec((rows, depth), lambda j: (0, 0)),
            pl.BlockSpec((1, depth, tile), lambda j: (0, 0, j)),
            pl.BlockSpec((1, depth, tile), lambda j: (0, 0, j)),
        ],
        out_specs=pl.BlockSpec((rows, tile), lambda j: (0, j)),
        compiler_params=pltpu.CompilerParams(vmem_limit_bytes=24 * 1024 * 1024),
        cost_estimate=pl.CostEstimate(
            flops=4 * rows * depth * hidden,
            bytes_accessed=4 * depth * hidden + 2 * rows * depth,
            transcendentals=rows * hidden,
        ),
    )(x, w_gate, w_up)


def down_kernel(a_ref, w_ref, o_ref):
    o_ref[...] = jnp.dot(a_ref[...], w_ref[0], preferred_element_type=jnp.float32).astype(
        jnp.bfloat16
    )


def down_add_kernel(a_ref, w_ref, other_ref, *refs):
    part = jnp.dot(a_ref[...], w_ref[0], preferred_element_type=jnp.float32)
    part = part.astype(jnp.bfloat16).astype(jnp.float32)
    refs[-1][...] = (part + other_ref[...].astype(jnp.float32)).astype(jnp.bfloat16)


def down(activation, w_down, side, added=None, into=None, tile=1024):
    rows, hidden = activation.shape
    width = w_down.shape[2]
    steps = width // 2 // tile
    first = side * steps
    in_specs = [
        pl.BlockSpec((rows, hidden), lambda j: (0, 0)),
        pl.BlockSpec((1, hidden, tile), lambda j: (0, 0, j + first)),
    ]
    args = [activation, w_down]
    aliases = {}
    if added is None:
        kernel, out_width, place = down_kernel, width // 2, 0
    else:
        kernel, out_width, place = down_add_kernel, width, first
        in_specs.append(pl.BlockSpec((rows, tile), lambda j: (0, j)))
        args.append(added)
        if into is not None:
            in_specs.append(pl.BlockSpec(memory_space=pl.ANY))
            args.append(into)
            aliases = {3: 0}
    return pl.pallas_call(
        kernel,
        out_shape=jax.ShapeDtypeStruct((rows, out_width), jnp.bfloat16),
        grid=(steps,),
        in_specs=in_specs,
        out_specs=pl.BlockSpec((rows, tile), lambda j: (0, j + place)),
        input_output_aliases=aliases,
        compiler_params=pltpu.CompilerParams(vmem_limit_bytes=16 * 1024 * 1024),
        cost_estimate=pl.CostEstimate(
            flops=rows * hidden * width,
            bytes_accessed=hidden * width + rows * width,
            transcendentals=0,
        ),
    )(*args)


def local(
    queries,
    rotated_key_rows,
    value_row_matrix,
    out_weight,
    residual,
    norm_gain,
    expert_ids,
    gate_weights,
    w_gate,
    w_up,
    w_down,
):
    bf16, f32 = jnp.bfloat16, jnp.float32
    rows = queries.shape[0]
    width = residual.shape[1]
    ring = lax.axis_size("y")
    experts = lax.axis_size("group") * ring
    y, core = lax.axis_index("y"), lax.axis_index("core")
    other = 1 - core
    chip_width = queries.shape[1] // ring
    half_width = chip_width // 2
    half = width // 2

    def along(value, step):
        return lax.ppermute(value, "y", [(i, (i + step) % ring) for i in range(ring)])

    def swap(value):
        return lax.ppermute(value, "core", [(0, 1), (1, 0)])

    def columns(value, start, size):
        return lax.dynamic_slice_in_dim(value, start, size, axis=1)

    weight_other = swap(out_weight)

    def outgoing(step):
        to = (y + step) % ring
        key_head = to * rotated_key_rows.shape[1] // HEAD // ring * HEAD
        return jnp.concatenate(
            [
                columns(queries, to * chip_width + core * half_width, half_width),
                columns(queries, to * chip_width + other * half_width, half_width),
                columns(rotated_key_rows, key_head, HEAD),
                columns(value_row_matrix, key_head, HEAD),
            ],
            axis=1,
        )

    arrived = {step: along(outgoing(step), step) for step in (2, 1, 3)}
    arrived[0] = outgoing(0)
    blocks = [arrived[(-s) % ring] for s in ORDER]
    key_values = jnp.stack([arrived[(-step) % ring][:, chip_width:] for step in range(ring)])
    key_values_other = swap(key_values)
    gathered = jnp.where(
        core == 0,
        jnp.stack([key_values, key_values_other], axis=1),
        jnp.stack([key_values_other, key_values], axis=1),
    )
    gathered = jnp.stack(
        [
            lax.dynamic_index_in_dim(gathered, (place - y) % ring, axis=0, keepdims=False)
            for place in range(ring)
        ]
    )
    gathered = gathered.reshape(ring * 2 * rows, 2 * HEAD)
    keys = gathered[:, :HEAD]
    values = jnp.concatenate([gathered[:, HEAD:], jnp.ones_like(keys)], axis=1)

    def attend(first, last):
        places = [(y + step) % ring for step in ORDER[first:last]]
        places = places + [places[0]] * (ring - len(places)) + [core]
        context = jnp.stack([block[:, :chip_width] for block in blocks[first:last]])
        return jnp.stack(places).astype(jnp.int32), context

    where, block = attend(0, 1)
    opposite = project(attention(where, block, keys, values), out_weight, weight_other, bf16)
    from_left = along(opposite[:, :half], 1)
    from_right = along(opposite[:, half:], -1)
    where, block = attend(1, 3)
    block, opposite = lax.optimization_barrier((block, opposite))
    partial = project(attention(where, block, keys, values), out_weight, weight_other, bf16)
    right, left = partial[:rows], partial[rows:]
    right_plain = along(right[:, half:], 1)
    left_plain = along(left[:, :half], -1)
    right_sum = along((right[:, :half].astype(f32) + from_left.astype(f32)).astype(bf16), 1)
    left_sum = along((left[:, half:].astype(f32) + from_right.astype(f32)).astype(bf16), -1)
    where, block = attend(3, 4)
    block, partial = lax.optimization_barrier((block, partial))
    own = project(attention(where, block, keys, values), out_weight, weight_other, f32)
    hidden = residual.astype(f32) + own
    hidden = hidden + jnp.concatenate(
        [
            right_sum.astype(f32) + left_plain.astype(f32),
            right_plain.astype(f32) + left_sum.astype(f32),
        ],
        axis=1,
    )

    mean_square = jnp.mean(hidden * hidden, axis=-1, keepdims=True)
    moe_input = (hidden * lax.rsqrt(mean_square + 1e-06) * norm_gain).astype(bf16)

    flat_ids = expert_ids.reshape(-1)
    one_hot = (flat_ids[:, None] == jnp.arange(experts, dtype=jnp.int32)[None, :]).astype(jnp.int32)
    earlier = jnp.cumsum(one_hot, axis=0) - one_hot
    rank_within = jnp.sum(earlier * one_hot, axis=1)
    slot_index = (flat_ids * CAP + rank_within).reshape(rows, TOP)
    slot_rows = jnp.arange(experts * CAP, dtype=jnp.int32)
    hit = [slot_rows[:, None] == slot_index[:, k][None, :] for k in range(TOP)]
    selector = (hit[0] | hit[1] | hit[2]).astype(bf16)
    spread = sum(
        jnp.where(slot_rows[None, :] == slot_index[:, k][:, None], gate_weights[:, k][:, None], 0.0)
        for k in range(TOP)
    )
    spread_high = spread.astype(bf16)
    spread_low = (spread - spread_high.astype(f32)).astype(bf16)

    slots = fdot(selector, moe_input).astype(bf16).reshape(experts, CAP, width)
    mine = lax.all_to_all(slots, ("group", "y"), split_axis=0, concat_axis=0, tiled=True)
    mine = mine.reshape(experts * CAP, width)
    theirs = swap(mine)

    active_mine = gated(mine, w_gate, w_up)
    theirs, active_mine = lax.optimization_barrier((theirs, active_mine))
    active_theirs = gated(theirs, w_gate, w_up)
    back = [swap(down(active_theirs, w_down, side)) for side in (0, 1)]
    expert_out = down(active_mine, w_down, 0, back[0])
    expert_out = down(active_mine, w_down, 1, back[1], expert_out)
    returned = lax.all_to_all(
        expert_out.reshape(experts, CAP, width),
        ("group", "y"),
        split_axis=0,
        concat_axis=0,
        tiled=True,
    ).reshape(experts * CAP, width)
    routed = fdot(spread_high, returned) + fdot(spread_low, returned)
    return (hidden + routed).astype(bf16)


def solution(mesh):
    devices = mesh.devices
    mesh = Mesh(devices.reshape(devices.shape[0], devices.shape[1] // 2, 2), AXES)
    wide = P(AXES, None)
    deep = P(AXES, None, None)
    return jax.shard_map(
        local,
        mesh=mesh,
        in_specs=(
            wide,
            wide,
            wide,
            P(("y", "core"), None),
            wide,
            P(),
            wide,
            wide,
            deep,
            deep,
            deep,
        ),
        out_specs=wide,
        check_vma=False,
    )
```

```python
import functools

import jax
import jax.numpy as jnp
from jax import lax
from jax.experimental import pallas as pl
from jax.experimental.pallas import tpu as pltpu
from jax.sharding import Mesh
from jax.sharding import PartitionSpec as P

HEAD = 128
TOP = 3
CAP = 8
AXES = ("group", "y", "core")
LOG2E = 1.4426950408889634
ORDER = (2, 1, 3, 0)


def attend(place, core, q_ref, k_ref, v_ref, context_ref, first):
    rows = q_ref.shape[1]
    heads = q_ref.shape[2] // HEAD
    scale = HEAD ** (-0.5) * LOG2E
    for block in range(4):

        @pl.when(place == block)
        def _():
            columns = 256 * (block + 1)
            keys = k_ref[0:columns, :]
            values = v_ref[0:columns, :]
            row = lax.broadcasted_iota(jnp.int32, (2 * rows, 256), 0) % rows
            column = lax.broadcasted_iota(jnp.int32, (2 * rows, 256), 1)
            allowed = column <= row + core * rows
            for index in range(heads // 2):
                start = index * 2 * HEAD
                both = q_ref[first, :, start : start + 2 * HEAD]
                q = jnp.concatenate([both[:, :HEAD], both[:, HEAD:]], axis=0)
                scores = lax.dot_general(
                    q, keys, (((1,), (1,)), ((), ())), preferred_element_type=jnp.float32
                )
                last = jnp.where(allowed, scores[:, columns - 256 :], -1e30)
                if block:
                    scores = jnp.concatenate([scores[:, : columns - 256], last], axis=1)
                else:
                    scores = last
                largest = jnp.max(scores, axis=1, keepdims=True)
                weights = jnp.exp2((scores - largest) * scale).astype(jnp.bfloat16)
                context = jnp.dot(weights, values, preferred_element_type=jnp.float32)
                context = (context[:, :HEAD] / context[:, HEAD:]).astype(jnp.bfloat16)
                context_ref[first * rows : (first + 1) * rows, start : start + 2 * HEAD] = (
                    jnp.concatenate([context[:rows], context[rows:]], axis=1)
                )


def attend_project_kernel(
    where_ref, q_ref, k_ref, v_ref, own_ref, other_ref, o_ref, context_ref
):
    @pl.when(pl.program_id(0) == 0)
    def _():
        for first in range(q_ref.shape[0]):
            attend(where_ref[first], where_ref[4], q_ref, k_ref, v_ref, context_ref, first)

    half = own_ref.shape[0]
    result = jnp.dot(
        context_ref[:, :half], own_ref[...], preferred_element_type=jnp.float32
    ) + jnp.dot(context_ref[:, half:], other_ref[...], preferred_element_type=jnp.float32)
    o_ref[...] = result.astype(o_ref.dtype)


def attend_project(where, queries, keys, values, weight_own, weight_other, dtype, tile=1024):
    ring, rows, depth = queries.shape
    half, width = weight_own.shape
    return pl.pallas_call(
        attend_project_kernel,
        out_shape=jax.ShapeDtypeStruct((ring * rows, width), dtype),
        grid_spec=pltpu.PrefetchScalarGridSpec(
            num_scalar_prefetch=1,
            grid=(width // tile,),
            in_specs=[
                pl.BlockSpec(queries.shape, lambda j, w: (0, 0, 0)),
                pl.BlockSpec(keys.shape, lambda j, w: (0, 0)),
                pl.BlockSpec(values.shape, lambda j, w: (0, 0)),
                pl.BlockSpec((half, tile), lambda j, w: (0, j)),
                pl.BlockSpec((half, tile), lambda j, w: (0, j)),
            ],
            out_specs=pl.BlockSpec((ring * rows, tile), lambda j, w: (0, j)),
            scratch_shapes=[pltpu.VMEM((ring * rows, depth), jnp.bfloat16)],
        ),
        compiler_params=pltpu.CompilerParams(vmem_limit_bytes=24 * 1024 * 1024),
        cost_estimate=pl.CostEstimate(
            flops=ring * rows * (2 * depth * width + 8 * 2560 * HEAD),
            bytes_accessed=2 * depth * width,
            transcendentals=ring * 2 * rows * 2560,
        ),
    )(where, queries, keys, values, weight_own, weight_other)


def fdot(a, b):
    return jnp.dot(a, b, preferred_element_type=jnp.float32)


def gated_kernel(tile, x_ref, gate_ref, up_ref, o_ref):
    for start in range(0, o_ref.shape[1], tile):
        at = slice(start, start + tile)
        gate = jnp.dot(x_ref[...], gate_ref[0, :, at], preferred_element_type=jnp.float32)
        upward = jnp.dot(x_ref[...], up_ref[0, :, at], preferred_element_type=jnp.float32)
        o_ref[:, at] = (gate / (1.0 + jnp.exp(-gate)) * upward).astype(jnp.bfloat16)


def gated(x, w_gate, w_up, tile=256):
    rows, depth = x.shape
    hidden = w_gate.shape[2]
    return pl.pallas_call(
        functools.partial(gated_kernel, tile),
        out_shape=jax.ShapeDtypeStruct((rows, hidden), jnp.bfloat16),
        in_specs=[pl.BlockSpec(memory_space=pltpu.VMEM)] * 3,
        out_specs=pl.BlockSpec(memory_space=pltpu.VMEM),
        compiler_params=pltpu.CompilerParams(vmem_limit_bytes=24 * 1024 * 1024),
        cost_estimate=pl.CostEstimate(
            flops=4 * rows * depth * hidden,
            bytes_accessed=4 * depth * hidden + 2 * rows * depth,
            transcendentals=rows * hidden,
        ),
    )(x, w_gate, w_up)


def down_kernel(tile, side, place, a_ref, w_ref, *refs):
    o_ref = refs[-1]
    half = w_ref.shape[2] // 2
    for start in range(0, half, tile):
        column = side * half + start
        part = jnp.dot(
            a_ref[...], w_ref[0, :, column : column + tile], preferred_element_type=jnp.float32
        ).astype(jnp.bfloat16)
        if len(refs) > 1:
            added = refs[0][:, start : start + tile].astype(jnp.float32)
            part = (part.astype(jnp.float32) + added).astype(jnp.bfloat16)
        o_ref[:, place + start : place + start + tile] = part


def down(activation, w_down, side, added=None, into=None, tile=512):
    rows, hidden = activation.shape
    width = w_down.shape[2]
    whole = added is not None
    args = [a for a in (activation, w_down, added, into) if a is not None]
    return pl.pallas_call(
        functools.partial(down_kernel, tile, side, side * width // 2 if whole else 0),
        out_shape=jax.ShapeDtypeStruct((rows, width if whole else width // 2), jnp.bfloat16),
        in_specs=[pl.BlockSpec(memory_space=pltpu.VMEM)] * len(args),
        out_specs=pl.BlockSpec(memory_space=pltpu.VMEM),
        input_output_aliases={3: 0} if into is not None else {},
        compiler_params=pltpu.CompilerParams(vmem_limit_bytes=16 * 1024 * 1024),
        cost_estimate=pl.CostEstimate(
            flops=rows * hidden * width,
            bytes_accessed=hidden * width + rows * width,
            transcendentals=0,
        ),
    )(*args)


def local(
    queries,
    rotated_key_rows,
    value_row_matrix,
    out_weight,
    residual,
    norm_gain,
    expert_ids,
    gate_weights,
    w_gate,
    w_up,
    w_down,
):
    bf16, f32 = jnp.bfloat16, jnp.float32
    rows = queries.shape[0]
    width = residual.shape[1]
    ring = lax.axis_size("y")
    experts = lax.axis_size("group") * ring
    y, core = lax.axis_index("y"), lax.axis_index("core")
    other = 1 - core
    chip_width = queries.shape[1] // ring
    half_width = chip_width // 2
    half = width // 2

    def along(value, step):
        return lax.ppermute(value, "y", [(i, (i + step) % ring) for i in range(ring)])

    def swap(value):
        return lax.ppermute(value, "core", [(0, 1), (1, 0)])

    def columns(value, start, size):
        return lax.dynamic_slice_in_dim(value, start, size, axis=1)

    weight_other = swap(out_weight)

    def head_rows(step):
        to = (y + step) % ring
        start = to * rotated_key_rows.shape[1] // HEAD // ring * HEAD
        return jnp.concatenate(
            [columns(rotated_key_rows, start, HEAD), columns(value_row_matrix, start, HEAD)], axis=1
        )

    def head_queries(step):
        start = (y + step) % ring * chip_width
        return jnp.concatenate(
            [
                columns(queries, start + core * half_width, half_width),
                columns(queries, start + other * half_width, half_width),
            ],
            axis=1,
        )

    to_send = {step: head_rows(step) for step in range(ring)}
    arrived = {(-step) % ring: along(to_send[step], step) for step in (2, 1, 3)}
    arrived[0] = to_send[0]
    asked = {2: along(head_queries(2), 2)}
    key_values = jnp.stack([arrived[step] for step in range(ring)])
    key_values_other = swap(key_values)
    near = [head_queries(1), head_queries(3)]
    near, key_values_other = lax.optimization_barrier((near, key_values_other))
    asked[3] = along(near[0], 1)
    asked[1] = along(near[1], 3)
    asked[0] = head_queries(0)
    blocks = [asked[step] for step in ORDER]
    gathered = jnp.where(
        core == 0,
        jnp.stack([key_values, key_values_other], axis=1),
        jnp.stack([key_values_other, key_values], axis=1),
    )
    gathered = jnp.stack(
        [
            lax.dynamic_index_in_dim(gathered, (place - y) % ring, axis=0, keepdims=False)
            for place in range(ring)
        ]
    )
    gathered = gathered.reshape(ring * 2 * rows, 2 * HEAD)
    keys = gathered[:, :HEAD]
    values = jnp.concatenate([gathered[:, HEAD:], jnp.ones_like(keys)], axis=1)

    def attended(first, last, block, dtype):
        places = [(y + step) % ring for step in ORDER[first:last]]
        places = places + [places[0]] * (ring - len(places)) + [core]
        places = jnp.stack(places).astype(jnp.int32)
        return attend_project(places, block, keys, values, out_weight, weight_other, dtype)

    opposite = attended(0, 1, jnp.stack(blocks[:1]), bf16)
    from_left = along(opposite[:, :half], 1)
    from_right = along(opposite[:, half:], -1)
    near, opposite = lax.optimization_barrier((blocks[1:3], opposite))
    near = jnp.stack(near)
    partial = attended(1, 3, near, bf16)
    right, left = partial[:rows], partial[rows:]
    right_plain = along(right[:, half:], 1)
    left_plain = along(left[:, :half], -1)
    from_left, from_right, partial = lax.optimization_barrier((from_left, from_right, partial))
    right_sum = along((partial[:rows, :half].astype(f32) + from_left.astype(f32)).astype(bf16), 1)
    left_sum = along((partial[rows:, half:].astype(f32) + from_right.astype(f32)).astype(bf16), -1)
    last, _ = lax.optimization_barrier((jnp.stack(blocks[3:]), partial))
    own = attended(3, 4, last, f32)
    hidden = residual.astype(f32) + own
    hidden = hidden + jnp.concatenate(
        [
            right_sum.astype(f32) + left_plain.astype(f32),
            right_plain.astype(f32) + left_sum.astype(f32),
        ],
        axis=1,
    )

    mean_square = jnp.mean(hidden * hidden, axis=-1, keepdims=True)
    moe_input = (hidden * lax.rsqrt(mean_square + 1e-06) * norm_gain).astype(bf16)

    flat_ids = expert_ids.reshape(-1)
    one_hot = (flat_ids[:, None] == jnp.arange(experts, dtype=jnp.int32)[None, :]).astype(jnp.int32)
    earlier = jnp.cumsum(one_hot, axis=0) - one_hot
    rank_within = jnp.sum(earlier * one_hot, axis=1)
    slot_index = (flat_ids * CAP + rank_within).reshape(rows, TOP)
    slot_rows = jnp.arange(experts * CAP, dtype=jnp.int32)
    hit = [slot_rows[:, None] == slot_index[:, k][None, :] for k in range(TOP)]
    selector = (hit[0] | hit[1] | hit[2]).astype(bf16)
    spread = sum(
        jnp.where(slot_rows[None, :] == slot_index[:, k][:, None], gate_weights[:, k][:, None], 0.0)
        for k in range(TOP)
    )
    spread_high = spread.astype(bf16)
    spread_low = (spread - spread_high.astype(f32)).astype(bf16)
    spread = jnp.concatenate([spread_high, spread_low], axis=0)

    slots = fdot(selector, moe_input).astype(bf16).reshape(experts, CAP, width)
    mine = lax.all_to_all(slots, ("group", "y"), split_axis=0, concat_axis=0, tiled=True)
    mine = mine.reshape(experts * CAP, width)
    theirs = swap(mine)

    active_mine = gated(mine, w_gate, w_up)
    theirs, active_mine = lax.optimization_barrier((theirs, active_mine))
    active_theirs = gated(theirs, w_gate, w_up)
    back = [swap(down(active_theirs, w_down, side)) for side in (0, 1)]
    expert_out = down(active_mine, w_down, 0, back[0])
    expert_out = down(active_mine, w_down, 1, back[1], expert_out)
    expert_out, spread, hidden = lax.optimization_barrier((expert_out, spread, hidden))
    returned = lax.all_to_all(
        expert_out.reshape(experts, CAP, width),
        ("group", "y"),
        split_axis=0,
        concat_axis=0,
        tiled=True,
    ).reshape(experts * CAP, width)
    routed = fdot(spread, returned)
    return (hidden + routed[:rows] + routed[rows:]).astype(bf16)


def solution(mesh):
    devices = mesh.devices
    mesh = Mesh(devices.reshape(devices.shape[0], devices.shape[1] // 2, 2), AXES)
    wide = P(AXES, None)
    deep = P(AXES, None, None)
    return jax.shard_map(
        local,
        mesh=mesh,
        in_specs=(
            wide,
            wide,
            wide,
            P(("y", "core"), None),
            wide,
            P(),
            wide,
            wide,
            deep,
            deep,
            deep,
        ),
        out_specs=wide,
        check_vma=False,
    )
```

```python
import functools

import jax
import jax.numpy as jnp
from jax import lax
from jax.experimental import pallas as pl
from jax.experimental.pallas import tpu as pltpu
from jax.sharding import Mesh
from jax.sharding import PartitionSpec as P

HEAD = 128
TOP = 3
CAP = 8
AXES = ("group", "y", "core")
LOG2E = 1.4426950408889634
ORDER = (2, 1, 3, 0)


def attend(place, core, q_ref, k_ref, v_ref, context_ref, first, unroll):
    rows = q_ref.shape[1]
    heads = q_ref.shape[2] // HEAD
    scale = HEAD ** (-0.5) * LOG2E
    for block in range(4):

        @pl.when(place == block)
        def _():
            columns = 256 * (block + 1)
            keys = k_ref[0:columns, :]
            values = v_ref[0:columns, :]
            row = lax.broadcasted_iota(jnp.int32, (2 * rows, 256), 0) % rows
            column = lax.broadcasted_iota(jnp.int32, (2 * rows, 256), 1)
            allowed = column <= row + core * rows
            def pair(index, carry):
                start = pl.multiple_of(index * 2 * HEAD, 2 * HEAD)
                both = q_ref[first, :, pl.ds(start, 2 * HEAD)]
                q = jnp.concatenate([both[:, :HEAD], both[:, HEAD:]], axis=0)
                scores = lax.dot_general(
                    q, keys, (((1,), (1,)), ((), ())), preferred_element_type=jnp.float32
                )
                last = jnp.where(allowed, scores[:, columns - 256 :], -1e30)
                if block:
                    scores = jnp.concatenate([scores[:, : columns - 256], last], axis=1)
                else:
                    scores = last
                largest = jnp.max(scores, axis=1, keepdims=True)
                weights = jnp.exp2((scores - largest) * scale).astype(jnp.bfloat16)
                context = jnp.dot(weights, values, preferred_element_type=jnp.float32)
                context = (context[:, :HEAD] / context[:, HEAD:]).astype(jnp.bfloat16)
                context_ref[pl.ds(first * rows, rows), pl.ds(start, 2 * HEAD)] = jnp.concatenate(
                    [context[:rows], context[rows:]], axis=1
                )
                return carry

            lax.fori_loop(0, heads // 2, pair, 0, unroll=unroll)


def attend_project_kernel(
    unroll, where_ref, q_ref, k_ref, v_ref, own_ref, other_ref, o_ref, context_ref
):
    @pl.when(pl.program_id(0) == 0)
    def _():
        @pl.loop(0, q_ref.shape[0])
        def _(first):
            attend(where_ref[first], where_ref[4], q_ref, k_ref, v_ref, context_ref, first, unroll)

    half = own_ref.shape[0]
    result = jnp.dot(
        context_ref[:, :half], own_ref[...], preferred_element_type=jnp.float32
    ) + jnp.dot(context_ref[:, half:], other_ref[...], preferred_element_type=jnp.float32)
    o_ref[...] = result.astype(o_ref.dtype)


def attend_project(where, queries, keys, values, weight_own, weight_other, dtype, unroll, tile=1024):
    ring, rows, depth = queries.shape
    half, width = weight_own.shape
    return pl.pallas_call(
        functools.partial(attend_project_kernel, unroll),
        out_shape=jax.ShapeDtypeStruct((ring * rows, width), dtype),
        grid_spec=pltpu.PrefetchScalarGridSpec(
            num_scalar_prefetch=1,
            grid=(width // tile,),
            in_specs=[
                pl.BlockSpec(queries.shape, lambda j, w: (0, 0, 0)),
                pl.BlockSpec(keys.shape, lambda j, w: (0, 0)),
                pl.BlockSpec(values.shape, lambda j, w: (0, 0)),
                pl.BlockSpec((half, tile), lambda j, w: (0, j)),
                pl.BlockSpec((half, tile), lambda j, w: (0, j)),
            ],
            out_specs=pl.BlockSpec((ring * rows, tile), lambda j, w: (0, j)),
            scratch_shapes=[pltpu.VMEM((ring * rows, depth), jnp.bfloat16)],
        ),
        compiler_params=pltpu.CompilerParams(vmem_limit_bytes=24 * 1024 * 1024),
        cost_estimate=pl.CostEstimate(
            flops=ring * rows * (2 * depth * width + 8 * 2560 * HEAD),
            bytes_accessed=2 * depth * width,
            transcendentals=ring * 2 * rows * 2560,
        ),
    )(where, queries, keys, values, weight_own, weight_other)


def fdot(a, b):
    return jnp.dot(a, b, preferred_element_type=jnp.float32)


def gated_kernel(tile, x_ref, gate_ref, up_ref, o_ref):
    @pl.loop(0, o_ref.shape[1] // tile)
    def _(step):
        at = pl.ds(pl.multiple_of(step * tile, tile), tile)
        gate = jnp.dot(x_ref[...], gate_ref[0, :, at], preferred_element_type=jnp.float32)
        upward = jnp.dot(x_ref[...], up_ref[0, :, at], preferred_element_type=jnp.float32)
        o_ref[:, at] = (gate / (1.0 + jnp.exp(-gate)) * upward).astype(jnp.bfloat16)


def gated(x, w_gate, w_up, tile=256):
    rows, depth = x.shape
    hidden = w_gate.shape[2]
    return pl.pallas_call(
        functools.partial(gated_kernel, tile),
        out_shape=jax.ShapeDtypeStruct((rows, hidden), jnp.bfloat16),
        in_specs=[pl.BlockSpec(memory_space=pltpu.VMEM)] * 3,
        out_specs=pl.BlockSpec(memory_space=pltpu.VMEM),
        compiler_params=pltpu.CompilerParams(vmem_limit_bytes=24 * 1024 * 1024),
        cost_estimate=pl.CostEstimate(
            flops=4 * rows * depth * hidden,
            bytes_accessed=4 * depth * hidden + 2 * rows * depth,
            transcendentals=rows * hidden,
        ),
    )(x, w_gate, w_up)


def down_kernel(tile, side, place, a_ref, w_ref, *refs):
    o_ref = refs[-1]
    half = w_ref.shape[2] // 2

    @pl.loop(0, half // tile, unroll=True)
    def _(step):
        start = pl.multiple_of(step * tile, tile)
        part = jnp.dot(
            a_ref[...],
            w_ref[0, :, pl.ds(start + side * half, tile)],
            preferred_element_type=jnp.float32,
        ).astype(jnp.bfloat16)
        if len(refs) > 1:
            added = refs[0][:, pl.ds(start, tile)].astype(jnp.float32)
            part = (part.astype(jnp.float32) + added).astype(jnp.bfloat16)
        o_ref[:, pl.ds(start + place, tile)] = part


def down(activation, w_down, side, added=None, into=None, tile=512):
    rows, hidden = activation.shape
    width = w_down.shape[2]
    whole = added is not None
    args = [a for a in (activation, w_down, added, into) if a is not None]
    return pl.pallas_call(
        functools.partial(down_kernel, tile, side, side * width // 2 if whole else 0),
        out_shape=jax.ShapeDtypeStruct((rows, width if whole else width // 2), jnp.bfloat16),
        in_specs=[pl.BlockSpec(memory_space=pltpu.VMEM)] * len(args),
        out_specs=pl.BlockSpec(memory_space=pltpu.VMEM),
        input_output_aliases={3: 0} if into is not None else {},
        compiler_params=pltpu.CompilerParams(vmem_limit_bytes=16 * 1024 * 1024),
        cost_estimate=pl.CostEstimate(
            flops=rows * hidden * width,
            bytes_accessed=hidden * width + rows * width,
            transcendentals=0,
        ),
    )(*args)


def local(
    queries,
    rotated_key_rows,
    value_row_matrix,
    out_weight,
    residual,
    norm_gain,
    expert_ids,
    gate_weights,
    w_gate,
    w_up,
    w_down,
):
    bf16, f32 = jnp.bfloat16, jnp.float32
    rows = queries.shape[0]
    width = residual.shape[1]
    ring = lax.axis_size("y")
    experts = lax.axis_size("group") * ring
    y, core = lax.axis_index("y"), lax.axis_index("core")
    other = 1 - core
    chip_width = queries.shape[1] // ring
    half_width = chip_width // 2
    half = width // 2

    def along(value, step):
        return lax.ppermute(value, "y", [(i, (i + step) % ring) for i in range(ring)])

    def swap(value):
        return lax.ppermute(value, "core", [(0, 1), (1, 0)])

    def columns(value, start, size):
        return lax.dynamic_slice_in_dim(value, start, size, axis=1)

    weight_other = swap(out_weight)

    def head_rows(step):
        to = (y + step) % ring
        start = to * rotated_key_rows.shape[1] // HEAD // ring * HEAD
        return jnp.concatenate(
            [columns(rotated_key_rows, start, HEAD), columns(value_row_matrix, start, HEAD)], axis=1
        )

    def head_queries(step):
        start = (y + step) % ring * chip_width
        return jnp.concatenate(
            [
                columns(queries, start + core * half_width, half_width),
                columns(queries, start + other * half_width, half_width),
            ],
            axis=1,
        )

    to_send = {step: head_rows(step) for step in range(ring)}
    arrived = {(-step) % ring: along(to_send[step], step) for step in (2, 1, 3)}
    arrived[0] = to_send[0]
    asked = {2: along(head_queries(2), 2)}
    key_values = jnp.stack([arrived[step] for step in range(ring)])
    key_values_other = swap(key_values)
    near = [head_queries(1), head_queries(3)]
    near, key_values_other = lax.optimization_barrier((near, key_values_other))
    asked[3] = along(near[0], 1)
    asked[1] = along(near[1], 3)
    asked[0] = head_queries(0)
    blocks = [asked[step] for step in ORDER]
    gathered = jnp.where(
        core == 0,
        jnp.stack([key_values, key_values_other], axis=1),
        jnp.stack([key_values_other, key_values], axis=1),
    )
    gathered = jnp.stack(
        [
            lax.dynamic_index_in_dim(gathered, (place - y) % ring, axis=0, keepdims=False)
            for place in range(ring)
        ]
    )
    gathered = gathered.reshape(ring * 2 * rows, 2 * HEAD)
    keys = gathered[:, :HEAD]
    values = jnp.concatenate([gathered[:, HEAD:], jnp.ones_like(keys)], axis=1)

    def attended(first, last, block, dtype, unroll):
        places = [(y + step) % ring for step in ORDER[first:last]]
        places = places + [places[0]] * (ring - len(places)) + [core]
        places = jnp.stack(places).astype(jnp.int32)
        return attend_project(places, block, keys, values, out_weight, weight_other, dtype, unroll)

    opposite = attended(0, 1, jnp.stack(blocks[:1]), bf16, 4)
    from_left = along(opposite[:, :half], 1)
    from_right = along(opposite[:, half:], -1)
    near, opposite = lax.optimization_barrier((blocks[1:3], opposite))
    near = jnp.stack(near)
    partial = attended(1, 3, near, bf16, 2)
    right, left = partial[:rows], partial[rows:]
    right_plain = along(right[:, half:], 1)
    left_plain = along(left[:, :half], -1)
    from_left, from_right, partial = lax.optimization_barrier((from_left, from_right, partial))
    right_sum = along((partial[:rows, :half].astype(f32) + from_left.astype(f32)).astype(bf16), 1)
    left_sum = along((partial[rows:, half:].astype(f32) + from_right.astype(f32)).astype(bf16), -1)
    last, _ = lax.optimization_barrier((jnp.stack(blocks[3:]), partial))
    own = attended(3, 4, last, f32, 1)
    hidden = residual.astype(f32) + own
    hidden = hidden + jnp.concatenate(
        [
            right_sum.astype(f32) + left_plain.astype(f32),
            right_plain.astype(f32) + left_sum.astype(f32),
        ],
        axis=1,
    )

    mean_square = jnp.mean(hidden * hidden, axis=-1, keepdims=True)
    moe_input = (hidden * lax.rsqrt(mean_square + 1e-06) * norm_gain).astype(bf16)

    flat_ids = expert_ids.reshape(-1)
    one_hot = (flat_ids[:, None] == jnp.arange(experts, dtype=jnp.int32)[None, :]).astype(jnp.int32)
    earlier = jnp.cumsum(one_hot, axis=0) - one_hot
    rank_within = jnp.sum(earlier * one_hot, axis=1)
    slot_index = (flat_ids * CAP + rank_within).reshape(rows, TOP)
    slot_rows = jnp.arange(experts * CAP, dtype=jnp.int32)
    hit = [slot_rows[:, None] == slot_index[:, k][None, :] for k in range(TOP)]
    selector = (hit[0] | hit[1] | hit[2]).astype(bf16)
    spread = sum(
        jnp.where(slot_rows[None, :] == slot_index[:, k][:, None], gate_weights[:, k][:, None], 0.0)
        for k in range(TOP)
    )
    spread_high = spread.astype(bf16)
    spread_low = (spread - spread_high.astype(f32)).astype(bf16)
    spread = jnp.concatenate([spread_high, spread_low], axis=0)

    slots = fdot(selector, moe_input).astype(bf16).reshape(experts, CAP, width)
    mine = lax.all_to_all(slots, ("group", "y"), split_axis=0, concat_axis=0, tiled=True)
    mine = mine.reshape(experts * CAP, width)
    theirs = swap(mine)

    active_mine = gated(mine, w_gate, w_up)
    theirs, active_mine = lax.optimization_barrier((theirs, active_mine))
    active_theirs = gated(theirs, w_gate, w_up)
    back = [swap(down(active_theirs, w_down, side)) for side in (0, 1)]
    expert_out = down(active_mine, w_down, 0, back[0])
    expert_out = down(active_mine, w_down, 1, back[1], expert_out)
    expert_out, spread, hidden = lax.optimization_barrier((expert_out, spread, hidden))
    returned = lax.all_to_all(
        expert_out.reshape(experts, CAP, width),
        ("group", "y"),
        split_axis=0,
        concat_axis=0,
        tiled=True,
    ).reshape(experts * CAP, width)
    routed = fdot(spread, returned)
    return (hidden + routed[:rows] + routed[rows:]).astype(bf16)


def solution(mesh):
    devices = mesh.devices
    mesh = Mesh(devices.reshape(devices.shape[0], devices.shape[1] // 2, 2), AXES)
    wide = P(AXES, None)
    deep = P(AXES, None, None)
    return jax.shard_map(
        local,
        mesh=mesh,
        in_specs=(
            wide,
            wide,
            wide,
            P(("y", "core"), None),
            wide,
            P(),
            wide,
            wide,
            deep,
            deep,
            deep,
        ),
        out_specs=wide,
        check_vma=False,
    )
```

```python
import functools

import jax
import jax.numpy as jnp
from jax import lax
from jax.experimental import pallas as pl
from jax.experimental.pallas import tpu as pltpu
from jax.sharding import Mesh
from jax.sharding import PartitionSpec as P

HEAD = 128
TOP = 3
CAP = 8
AXES = ("group", "y", "core")
LOG2E = 1.4426950408889634
ORDER = (2, 1, 3, 0)
PARTS = 4


def attend(place, core, q_ref, k_ref, v_ref, context_ref, first, unroll):
    rows = q_ref.shape[1]
    heads = q_ref.shape[2] // HEAD
    scale = HEAD ** (-0.5) * LOG2E
    for block in range(4):

        @pl.when(place == block)
        def _():
            columns = 256 * (block + 1)
            keys = k_ref[0:columns, :]
            values = v_ref[0:columns, :]
            row = lax.broadcasted_iota(jnp.int32, (2 * rows, 256), 0) % rows
            column = lax.broadcasted_iota(jnp.int32, (2 * rows, 256), 1)
            allowed = column <= row + core * rows
            def pair(index, carry):
                start = pl.multiple_of(index * 2 * HEAD, 2 * HEAD)
                both = q_ref[first, :, pl.ds(start, 2 * HEAD)]
                q = jnp.concatenate([both[:, :HEAD], both[:, HEAD:]], axis=0)
                scores = lax.dot_general(
                    q, keys, (((1,), (1,)), ((), ())), preferred_element_type=jnp.float32
                )
                last = jnp.where(allowed, scores[:, columns - 256 :], -1e30)
                if block:
                    scores = jnp.concatenate([scores[:, : columns - 256], last], axis=1)
                else:
                    scores = last
                largest = jnp.max(scores, axis=1, keepdims=True)
                weights = jnp.exp2((scores - largest) * scale).astype(jnp.bfloat16)
                context = jnp.dot(weights, values, preferred_element_type=jnp.float32)
                context = (context[:, :HEAD] / context[:, HEAD:]).astype(jnp.bfloat16)
                context_ref[pl.ds(first * rows, rows), pl.ds(start, 2 * HEAD)] = jnp.concatenate(
                    [context[:rows], context[rows:]], axis=1
                )
                return carry

            lax.fori_loop(0, heads // 2, pair, 0, unroll=unroll)


def attend_project_kernel(
    unroll, where_ref, q_ref, k_ref, v_ref, own_ref, other_ref, o_ref, context_ref
):
    @pl.when(pl.program_id(0) == 0)
    def _():
        @pl.loop(0, q_ref.shape[0])
        def _(first):
            attend(where_ref[first], where_ref[4], q_ref, k_ref, v_ref, context_ref, first, unroll)

    half = own_ref.shape[0]
    result = jnp.dot(
        context_ref[:, :half], own_ref[...], preferred_element_type=jnp.float32
    ) + jnp.dot(context_ref[:, half:], other_ref[...], preferred_element_type=jnp.float32)
    o_ref[...] = result.astype(o_ref.dtype)


def attend_project(where, queries, keys, values, weight_own, weight_other, dtype, unroll, tile=1024):
    ring, rows, depth = queries.shape
    half, width = weight_own.shape
    return pl.pallas_call(
        functools.partial(attend_project_kernel, unroll),
        out_shape=jax.ShapeDtypeStruct((ring * rows, width), dtype),
        grid_spec=pltpu.PrefetchScalarGridSpec(
            num_scalar_prefetch=1,
            grid=(width // tile,),
            in_specs=[
                pl.BlockSpec(queries.shape, lambda j, w: (0, 0, 0)),
                pl.BlockSpec(keys.shape, lambda j, w: (0, 0)),
                pl.BlockSpec(values.shape, lambda j, w: (0, 0)),
                pl.BlockSpec((half, tile), lambda j, w: (0, j)),
                pl.BlockSpec((half, tile), lambda j, w: (0, j)),
            ],
            out_specs=pl.BlockSpec((ring * rows, tile), lambda j, w: (0, j)),
            scratch_shapes=[pltpu.VMEM((ring * rows, depth), jnp.bfloat16)],
        ),
        compiler_params=pltpu.CompilerParams(vmem_limit_bytes=24 * 1024 * 1024),
        cost_estimate=pl.CostEstimate(
            flops=ring * rows * (2 * depth * width + 8 * 2560 * HEAD),
            bytes_accessed=2 * depth * width,
            transcendentals=ring * 2 * rows * 2560,
        ),
    )(where, queries, keys, values, weight_own, weight_other)


def fdot(a, b):
    return jnp.dot(a, b, preferred_element_type=jnp.float32)


def gated_kernel(tile, x_ref, gate_ref, up_ref, o_ref):
    @pl.loop(0, o_ref.shape[1] // tile)
    def _(step):
        at = pl.ds(pl.multiple_of(step * tile, tile), tile)
        gate = jnp.dot(x_ref[...], gate_ref[0, :, at], preferred_element_type=jnp.float32)
        upward = jnp.dot(x_ref[...], up_ref[0, :, at], preferred_element_type=jnp.float32)
        o_ref[:, at] = (gate / (1.0 + jnp.exp(-gate)) * upward).astype(jnp.bfloat16)


def gated(x, w_gate, w_up, tile=256):
    rows, depth = x.shape
    hidden = w_gate.shape[2]
    return pl.pallas_call(
        functools.partial(gated_kernel, tile),
        out_shape=jax.ShapeDtypeStruct((rows, hidden), jnp.bfloat16),
        in_specs=[pl.BlockSpec(memory_space=pltpu.VMEM)] * 3,
        out_specs=pl.BlockSpec(memory_space=pltpu.VMEM),
        compiler_params=pltpu.CompilerParams(vmem_limit_bytes=24 * 1024 * 1024),
        cost_estimate=pl.CostEstimate(
            flops=4 * rows * depth * hidden,
            bytes_accessed=4 * depth * hidden + 2 * rows * depth,
            transcendentals=rows * hidden,
        ),
    )(x, w_gate, w_up)


def down_kernel(tile, side, place, a_ref, w_ref, *refs):
    o_ref = refs[-1]
    some = w_ref.shape[2] // PARTS

    @pl.loop(0, some // tile, unroll=True)
    def _(step):
        start = pl.multiple_of(step * tile, tile)
        part = jnp.dot(
            a_ref[...],
            w_ref[0, :, pl.ds(start + side * some, tile)],
            preferred_element_type=jnp.float32,
        ).astype(jnp.bfloat16)
        if len(refs) > 1:
            added = refs[0][:, pl.ds(start, tile)].astype(jnp.float32)
            part = (part.astype(jnp.float32) + added).astype(jnp.bfloat16)
        o_ref[:, pl.ds(start + place, tile)] = part


def down(activation, w_down, side, added=None, into=None, tile=512):
    rows, hidden = activation.shape
    width = w_down.shape[2]
    whole = added is not None
    args = [a for a in (activation, w_down, added, into) if a is not None]
    return pl.pallas_call(
        functools.partial(down_kernel, tile, side, side * width // PARTS if whole else 0),
        out_shape=jax.ShapeDtypeStruct((rows, width if whole else width // PARTS), jnp.bfloat16),
        in_specs=[pl.BlockSpec(memory_space=pltpu.VMEM)] * len(args),
        out_specs=pl.BlockSpec(memory_space=pltpu.VMEM),
        input_output_aliases={3: 0} if into is not None else {},
        compiler_params=pltpu.CompilerParams(vmem_limit_bytes=16 * 1024 * 1024),
        cost_estimate=pl.CostEstimate(
            flops=2 * rows * hidden * width // PARTS,
            bytes_accessed=2 * (hidden + rows) * width // PARTS,
            transcendentals=0,
        ),
    )(*args)


def local(
    queries,
    rotated_key_rows,
    value_row_matrix,
    out_weight,
    residual,
    norm_gain,
    expert_ids,
    gate_weights,
    w_gate,
    w_up,
    w_down,
):
    bf16, f32 = jnp.bfloat16, jnp.float32
    rows = queries.shape[0]
    width = residual.shape[1]
    ring = lax.axis_size("y")
    experts = lax.axis_size("group") * ring
    y, core = lax.axis_index("y"), lax.axis_index("core")
    other = 1 - core
    chip_width = queries.shape[1] // ring
    half_width = chip_width // 2
    half = width // 2

    def along(value, step):
        return lax.ppermute(value, "y", [(i, (i + step) % ring) for i in range(ring)])

    def swap(value):
        return lax.ppermute(value, "core", [(0, 1), (1, 0)])

    def columns(value, start, size):
        return lax.dynamic_slice_in_dim(value, start, size, axis=1)

    weight_other = swap(out_weight)

    def head_rows(step):
        to = (y + step) % ring
        start = to * rotated_key_rows.shape[1] // HEAD // ring * HEAD
        return jnp.concatenate(
            [columns(rotated_key_rows, start, HEAD), columns(value_row_matrix, start, HEAD)], axis=1
        )

    def head_queries(step):
        start = (y + step) % ring * chip_width
        return jnp.concatenate(
            [
                columns(queries, start + core * half_width, half_width),
                columns(queries, start + other * half_width, half_width),
            ],
            axis=1,
        )

    to_send = {step: head_rows(step) for step in range(ring)}
    asked = {2: along(head_queries(2), 2)}
    arrived = {(-step) % ring: along(to_send[step], step) for step in (2, 1, 3)}
    arrived[0] = to_send[0]
    key_values = jnp.stack([arrived[step] for step in range(ring)])
    key_values_other = swap(key_values)
    near = [head_queries(1), head_queries(3)]
    asked[3] = along(near[0], 1)
    asked[1] = along(near[1], 3)
    asked[0] = head_queries(0)
    blocks = [asked[step] for step in ORDER]
    gathered = jnp.where(
        core == 0,
        jnp.stack([key_values, key_values_other], axis=1),
        jnp.stack([key_values_other, key_values], axis=1),
    )
    gathered = jnp.stack(
        [
            lax.dynamic_index_in_dim(gathered, (place - y) % ring, axis=0, keepdims=False)
            for place in range(ring)
        ]
    )
    gathered = gathered.reshape(ring * 2 * rows, 2 * HEAD)
    keys = gathered[:, :HEAD]
    values = jnp.concatenate([gathered[:, HEAD:], jnp.ones_like(keys)], axis=1)

    def attended(first, last, block, dtype, unroll):
        places = [(y + step) % ring for step in ORDER[first:last]]
        places = places + [places[0]] * (ring - len(places)) + [core]
        places = jnp.stack(places).astype(jnp.int32)
        return attend_project(places, block, keys, values, out_weight, weight_other, dtype, unroll)

    opposite = attended(0, 1, jnp.stack(blocks[:1]), bf16, 4)
    from_left = along(opposite[:, :half], 1)
    from_right = along(opposite[:, half:], -1)
    near, opposite = lax.optimization_barrier((blocks[1:3], opposite))
    near = jnp.stack(near)
    partial = attended(1, 3, near, bf16, 2)
    right, left = partial[:rows], partial[rows:]
    right_plain = along(right[:, half:], 1)
    left_plain = along(left[:, :half], -1)
    from_left, from_right, partial = lax.optimization_barrier((from_left, from_right, partial))
    right_sum = along((partial[:rows, :half].astype(f32) + from_left.astype(f32)).astype(bf16), 1)
    left_sum = along((partial[rows:, half:].astype(f32) + from_right.astype(f32)).astype(bf16), -1)
    last, _ = lax.optimization_barrier((jnp.stack(blocks[3:]), partial))
    own = attended(3, 4, last, f32, 1)
    hidden = residual.astype(f32) + own
    hidden = hidden + jnp.concatenate(
        [
            right_sum.astype(f32) + left_plain.astype(f32),
            right_plain.astype(f32) + left_sum.astype(f32),
        ],
        axis=1,
    )

    mean_square = jnp.mean(hidden * hidden, axis=-1, keepdims=True)
    moe_input = (hidden * lax.rsqrt(mean_square + 1e-06) * norm_gain).astype(bf16)

    flat_ids = expert_ids.reshape(-1)
    one_hot = (flat_ids[:, None] == jnp.arange(experts, dtype=jnp.int32)[None, :]).astype(jnp.int32)
    earlier = jnp.cumsum(one_hot, axis=0) - one_hot
    rank_within = jnp.sum(earlier * one_hot, axis=1)
    slot_index = (flat_ids * CAP + rank_within).reshape(rows, TOP)
    slot_rows = jnp.arange(experts * CAP, dtype=jnp.int32)
    hit = [slot_rows[:, None] == slot_index[:, k][None, :] for k in range(TOP)]
    selector = (hit[0] | hit[1] | hit[2]).astype(bf16)
    spread = sum(
        jnp.where(slot_rows[None, :] == slot_index[:, k][:, None], gate_weights[:, k][:, None], 0.0)
        for k in range(TOP)
    )
    spread_high = spread.astype(bf16)
    spread_low = (spread - spread_high.astype(f32)).astype(bf16)
    spread = jnp.concatenate([spread_high, spread_low], axis=0)

    slots = fdot(selector, moe_input).astype(bf16).reshape(experts, CAP, width)
    slots, spread, hidden = lax.optimization_barrier((slots, spread, hidden))
    mine = lax.all_to_all(slots, ("group", "y"), split_axis=0, concat_axis=0, tiled=True)
    mine = mine.reshape(experts * CAP, width)
    theirs = swap(mine)

    active_mine = gated(mine, w_gate, w_up)
    theirs, active_mine = lax.optimization_barrier((theirs, active_mine))
    active_theirs = gated(theirs, w_gate, w_up)
    back = [swap(down(active_theirs, w_down, side)) for side in range(PARTS)]
    expert_out = None
    for side in range(PARTS):
        expert_out = down(active_mine, w_down, side, back[side], expert_out)
    expert_out, spread, hidden = lax.optimization_barrier((expert_out, spread, hidden))
    returned = lax.all_to_all(
        expert_out.reshape(experts, CAP, width),
        ("group", "y"),
        split_axis=0,
        concat_axis=0,
        tiled=True,
    ).reshape(experts * CAP, width)
    routed = fdot(spread, returned)
    return (hidden + routed[:rows] + routed[rows:]).astype(bf16)


def solution(mesh):
    devices = mesh.devices
    mesh = Mesh(devices.reshape(devices.shape[0], devices.shape[1] // 2, 2), AXES)
    wide = P(AXES, None)
    deep = P(AXES, None, None)
    return jax.shard_map(
        local,
        mesh=mesh,
        in_specs=(
            wide,
            wide,
            wide,
            P(("y", "core"), None),
            wide,
            P(),
            wide,
            wide,
            deep,
            deep,
            deep,
        ),
        out_specs=wide,
        check_vma=False,
    )
```

```python
import functools

import jax
import jax.numpy as jnp
from jax import lax
from jax.experimental import pallas as pl
from jax.experimental.pallas import tpu as pltpu
from jax.sharding import Mesh
from jax.sharding import PartitionSpec as P

HEAD = 128
TOP = 3
CAP = 8
AXES = ("group", "y", "core")
LOG2E = 1.4426950408889634
ORDER = (2, 1, 3, 0)
PARTS = 4


def attend(place, core, q_ref, k_ref, v_ref, context_ref, first, unroll):
    rows = q_ref.shape[1]
    heads = q_ref.shape[2] // HEAD
    scale = HEAD ** (-0.5) * LOG2E
    for block in range(4):

        @pl.when(place == block)
        def _():
            columns = 256 * (block + 1)
            keys = k_ref[0:columns, :]
            values = v_ref[0:columns, :]
            row = lax.broadcasted_iota(jnp.int32, (2 * rows, 256), 0) % rows
            column = lax.broadcasted_iota(jnp.int32, (2 * rows, 256), 1)
            allowed = column <= row + core * rows
            def pair(index, carry):
                start = pl.multiple_of(index * 2 * HEAD, 2 * HEAD)
                both = q_ref[first, :, pl.ds(start, 2 * HEAD)]
                q = jnp.concatenate([both[:, :HEAD], both[:, HEAD:]], axis=0)
                scores = lax.dot_general(
                    q, keys, (((1,), (1,)), ((), ())), preferred_element_type=jnp.float32
                )
                last = jnp.where(allowed, scores[:, columns - 256 :], -1e30)
                if block:
                    scores = jnp.concatenate([scores[:, : columns - 256], last], axis=1)
                else:
                    scores = last
                largest = jnp.max(scores, axis=1, keepdims=True)
                weights = jnp.exp2((scores - largest) * scale).astype(jnp.bfloat16)
                context = jnp.dot(weights, values, preferred_element_type=jnp.float32)
                context = (context[:, :HEAD] / context[:, HEAD:]).astype(jnp.bfloat16)
                context_ref[pl.ds(first * rows, rows), pl.ds(start, 2 * HEAD)] = jnp.concatenate(
                    [context[:rows], context[rows:]], axis=1
                )
                return carry

            lax.fori_loop(0, heads // 2, pair, 0, unroll=unroll)


def attend_project_kernel(
    unroll, where_ref, q_ref, k_ref, v_ref, own_ref, other_ref, o_ref, context_ref
):
    @pl.when(pl.program_id(0) == 0)
    def _():
        @pl.loop(0, q_ref.shape[0])
        def _(first):
            attend(where_ref[first], where_ref[4], q_ref, k_ref, v_ref, context_ref, first, unroll)

    half = own_ref.shape[0]
    result = jnp.dot(
        context_ref[:, :half], own_ref[...], preferred_element_type=jnp.float32
    ) + jnp.dot(context_ref[:, half:], other_ref[...], preferred_element_type=jnp.float32)
    o_ref[...] = result.astype(o_ref.dtype)


def attend_project(where, queries, keys, values, weight_own, weight_other, dtype, unroll, tile=1024):
    ring, rows, depth = queries.shape
    half, width = weight_own.shape
    return pl.pallas_call(
        functools.partial(attend_project_kernel, unroll),
        out_shape=jax.ShapeDtypeStruct((ring * rows, width), dtype),
        grid_spec=pltpu.PrefetchScalarGridSpec(
            num_scalar_prefetch=1,
            grid=(width // tile,),
            in_specs=[
                pl.BlockSpec(queries.shape, lambda j, w: (0, 0, 0)),
                pl.BlockSpec(keys.shape, lambda j, w: (0, 0)),
                pl.BlockSpec(values.shape, lambda j, w: (0, 0)),
                pl.BlockSpec((half, tile), lambda j, w: (0, j)),
                pl.BlockSpec((half, tile), lambda j, w: (0, j)),
            ],
            out_specs=pl.BlockSpec((ring * rows, tile), lambda j, w: (0, j)),
            scratch_shapes=[pltpu.VMEM((ring * rows, depth), jnp.bfloat16)],
        ),
        compiler_params=pltpu.CompilerParams(vmem_limit_bytes=24 * 1024 * 1024),
        cost_estimate=pl.CostEstimate(
            flops=ring * rows * (2 * depth * width + 8 * 2560 * HEAD),
            bytes_accessed=2 * depth * width,
            transcendentals=ring * 2 * rows * 2560,
        ),
    )(where, queries, keys, values, weight_own, weight_other)


def fdot(a, b):
    return jnp.dot(a, b, preferred_element_type=jnp.float32)


def gated_kernel(tile, unroll, x_ref, gate_ref, up_ref, o_ref):
    @pl.loop(0, o_ref.shape[1] // tile, unroll=unroll)
    def _(step):
        at = pl.ds(pl.multiple_of(step * tile, tile), tile)
        gate = jnp.dot(x_ref[...], gate_ref[0, :, at], preferred_element_type=jnp.float32)
        upward = jnp.dot(x_ref[...], up_ref[0, :, at], preferred_element_type=jnp.float32)
        o_ref[:, at] = (gate / (1.0 + jnp.exp(-gate)) * upward).astype(jnp.bfloat16)


def gated(x, w_gate, w_up, unroll, tile=256):
    rows, depth = x.shape
    hidden = w_gate.shape[2]
    return pl.pallas_call(
        functools.partial(gated_kernel, tile, unroll),
        out_shape=jax.ShapeDtypeStruct((rows, hidden), jnp.bfloat16),
        in_specs=[pl.BlockSpec(memory_space=pltpu.VMEM)] * 3,
        out_specs=pl.BlockSpec(memory_space=pltpu.VMEM),
        compiler_params=pltpu.CompilerParams(vmem_limit_bytes=24 * 1024 * 1024),
        cost_estimate=pl.CostEstimate(
            flops=4 * rows * depth * hidden,
            bytes_accessed=4 * depth * hidden + 2 * rows * depth,
            transcendentals=rows * hidden,
        ),
    )(x, w_gate, w_up)


def down_kernel(tile, side, place, a_ref, w_ref, *refs):
    o_ref = refs[-1]
    some = w_ref.shape[2] // PARTS

    @pl.loop(0, some // tile, unroll=True)
    def _(step):
        start = pl.multiple_of(step * tile, tile)
        part = jnp.dot(
            a_ref[...],
            w_ref[0, :, pl.ds(start + side * some, tile)],
            preferred_element_type=jnp.float32,
        ).astype(jnp.bfloat16)
        if len(refs) > 1:
            added = refs[0][:, pl.ds(start, tile)].astype(jnp.float32)
            part = (part.astype(jnp.float32) + added).astype(jnp.bfloat16)
        o_ref[:, pl.ds(start + place, tile)] = part


def down(activation, w_down, side, added=None, into=None, tile=512):
    rows, hidden = activation.shape
    width = w_down.shape[2]
    whole = added is not None
    args = [a for a in (activation, w_down, added, into) if a is not None]
    return pl.pallas_call(
        functools.partial(down_kernel, tile, side, side * width // PARTS if whole else 0),
        out_shape=jax.ShapeDtypeStruct((rows, width if whole else width // PARTS), jnp.bfloat16),
        in_specs=[pl.BlockSpec(memory_space=pltpu.VMEM)] * len(args),
        out_specs=pl.BlockSpec(memory_space=pltpu.VMEM),
        input_output_aliases={3: 0} if into is not None else {},
        compiler_params=pltpu.CompilerParams(vmem_limit_bytes=16 * 1024 * 1024),
        cost_estimate=pl.CostEstimate(
            flops=2 * rows * hidden * width // PARTS,
            bytes_accessed=2 * (hidden + rows) * width // PARTS,
            transcendentals=0,
        ),
    )(*args)


def local(
    queries,
    rotated_key_rows,
    value_row_matrix,
    out_weight,
    residual,
    norm_gain,
    expert_ids,
    gate_weights,
    w_gate,
    w_up,
    w_down,
):
    bf16, f32 = jnp.bfloat16, jnp.float32
    rows = queries.shape[0]
    width = residual.shape[1]
    ring = lax.axis_size("y")
    experts = lax.axis_size("group") * ring
    y, core = lax.axis_index("y"), lax.axis_index("core")
    other = 1 - core
    chip_width = queries.shape[1] // ring
    half_width = chip_width // 2
    half = width // 2

    def along(value, step):
        return lax.ppermute(value, "y", [(i, (i + step) % ring) for i in range(ring)])

    def swap(value):
        return lax.ppermute(value, "core", [(0, 1), (1, 0)])

    def columns(value, start, size):
        return lax.dynamic_slice_in_dim(value, start, size, axis=1)

    weight_other = swap(out_weight)

    def head_rows(step):
        to = (y + step) % ring
        start = to * rotated_key_rows.shape[1] // HEAD // ring * HEAD
        return jnp.concatenate(
            [columns(rotated_key_rows, start, HEAD), columns(value_row_matrix, start, HEAD)], axis=1
        )

    def head_queries(step):
        start = (y + step) % ring * chip_width
        return jnp.concatenate(
            [
                columns(queries, start + core * half_width, half_width),
                columns(queries, start + other * half_width, half_width),
            ],
            axis=1,
        )

    to_send = {step: head_rows(step) for step in range(ring)}
    asked = {2: along(head_queries(2), 2)}
    arrived = {(-step) % ring: along(to_send[step], step) for step in (2, 1, 3)}
    arrived[0] = to_send[0]
    key_values = jnp.stack([arrived[step] for step in range(ring)])
    key_values_other = swap(key_values)
    near = [head_queries(1), head_queries(3)]
    asked[3] = along(near[0], 1)
    asked[1] = along(near[1], 3)
    asked[0] = head_queries(0)
    blocks = [asked[step] for step in ORDER]
    gathered = jnp.where(
        core == 0,
        jnp.stack([key_values, key_values_other], axis=1),
        jnp.stack([key_values_other, key_values], axis=1),
    )
    gathered = jnp.stack(
        [
            lax.dynamic_index_in_dim(gathered, (place - y) % ring, axis=0, keepdims=False)
            for place in range(ring)
        ]
    )
    gathered = gathered.reshape(ring * 2 * rows, 2 * HEAD)
    keys = gathered[:, :HEAD]
    values = jnp.concatenate([gathered[:, HEAD:], jnp.ones_like(keys)], axis=1)

    def attended(first, last, block, dtype, unroll, tile=1024):
        places = [(y + step) % ring for step in ORDER[first:last]]
        places = places + [places[0]] * (ring - len(places)) + [core]
        places = jnp.stack(places).astype(jnp.int32)
        return attend_project(places, block, keys, values, out_weight, weight_other, dtype, unroll, tile)

    opposite = attended(0, 1, jnp.stack(blocks[:1]), bf16, 4)
    from_left = along(opposite[:, :half], 1)
    from_right = along(opposite[:, half:], -1)
    near, opposite = lax.optimization_barrier((blocks[1:3], opposite))
    near = jnp.stack(near)
    partial = attended(1, 3, near, bf16, 2)
    right, left = partial[:rows], partial[rows:]
    right_plain = along(right[:, half:], 1)
    left_plain = along(left[:, :half], -1)
    from_left, from_right, partial = lax.optimization_barrier((from_left, from_right, partial))
    right_sum = along((partial[:rows, :half].astype(f32) + from_left.astype(f32)).astype(bf16), 1)
    left_sum = along((partial[rows:, half:].astype(f32) + from_right.astype(f32)).astype(bf16), -1)
    last, _ = lax.optimization_barrier((jnp.stack(blocks[3:]), partial))
    own = attended(3, 4, last, f32, 1, 512)
    hidden = residual.astype(f32) + own
    hidden = hidden + jnp.concatenate(
        [
            right_sum.astype(f32) + left_plain.astype(f32),
            right_plain.astype(f32) + left_sum.astype(f32),
        ],
        axis=1,
    )

    mean_square = jnp.mean(hidden * hidden, axis=-1, keepdims=True)
    moe_input = (hidden * lax.rsqrt(mean_square + 1e-06) * norm_gain).astype(bf16)

    flat_ids = expert_ids.reshape(-1)
    one_hot = (flat_ids[:, None] == jnp.arange(experts, dtype=jnp.int32)[None, :]).astype(jnp.int32)
    earlier = jnp.cumsum(one_hot, axis=0) - one_hot
    rank_within = jnp.sum(earlier * one_hot, axis=1)
    slot_index = (flat_ids * CAP + rank_within).reshape(rows, TOP)
    slot_rows = jnp.arange(experts * CAP, dtype=jnp.int32)
    hit = [slot_rows[:, None] == slot_index[:, k][None, :] for k in range(TOP)]
    selector = (hit[0] | hit[1] | hit[2]).astype(bf16)
    spread = sum(
        jnp.where(slot_rows[None, :] == slot_index[:, k][:, None], gate_weights[:, k][:, None], 0.0)
        for k in range(TOP)
    )
    spread_high = spread.astype(bf16)
    spread_low = (spread - spread_high.astype(f32)).astype(bf16)
    spread = jnp.concatenate([spread_high, spread_low], axis=0)

    slots = fdot(selector, moe_input).astype(bf16).reshape(experts, CAP, width)
    slots, spread, hidden = lax.optimization_barrier((slots, spread, hidden))
    mine = lax.all_to_all(slots, ("group", "y"), split_axis=0, concat_axis=0, tiled=True)
    mine = mine.reshape(experts * CAP, width)
    theirs = swap(mine)

    active_mine = gated(mine, w_gate, w_up, 1)
    theirs, active_mine = lax.optimization_barrier((theirs, active_mine))
    active_theirs = gated(theirs, w_gate, w_up, 3)
    back = [swap(down(active_theirs, w_down, side)) for side in range(PARTS)]
    expert_out = None
    for side in range(PARTS):
        expert_out = down(active_mine, w_down, side, back[side], expert_out)
    expert_out, spread, hidden = lax.optimization_barrier((expert_out, spread, hidden))
    returned = lax.all_to_all(
        expert_out.reshape(experts, CAP, width),
        ("group", "y"),
        split_axis=0,
        concat_axis=0,
        tiled=True,
    ).reshape(experts * CAP, width)
    routed = fdot(spread, returned)
    return (hidden + routed[:rows] + routed[rows:]).astype(bf16)


def solution(mesh):
    devices = mesh.devices
    mesh = Mesh(devices.reshape(devices.shape[0], devices.shape[1] // 2, 2), AXES)
    wide = P(AXES, None)
    deep = P(AXES, None, None)
    return jax.shard_map(
        local,
        mesh=mesh,
        in_specs=(
            wide,
            wide,
            wide,
            P(("y", "core"), None),
            wide,
            P(),
            wide,
            wide,
            deep,
            deep,
            deep,
        ),
        out_specs=wide,
        check_vma=False,
    )
```
